32 devices in a mesh: patch: 2 (over x), visit: 16 (over z, y, core).
Axes of the slice: x: 2, y: 2, z: 4, core: 2. Of those that a mesh axis runs over, the one named last changes fastest.
Arguments:
- template: bfloat16 [1024, 8192], P('visit', 'patch'), may hold values from -6 to 6
- science: bfloat16 [1024, 8192], P('visit', 'patch'), may hold values from -6 to 6
- row_shift: int32 [16, 2], P('visit', 'patch'), may hold values from -22 to 22, as said below
- col_shift: int32 [16, 2], P('visit', 'patch'), may hold values from -1024 to 1024, as said below
- valid_rows: int32 [16, 2], P('visit', 'patch'), may hold values from 32 to 64
- basis_rows: bfloat16 [9, 21], replicated, may hold values from -2.5 to 2.5
- basis_cols: bfloat16 [9, 21], replicated, may hold values from -2.5 to 2.5
- kernel_terms: float32 [16, 2, 9], P('visit', 'patch'), may hold values from -2.5 to 2.5
Outputs:
- patch_difference: float32 [1024, 8192], P('visit', 'patch')
The draws below stay inside these ranges and needn't reach their ends.
Inputs may be any that keep to these rules, and one draw needn't show every extreme that they name: row_shift takes both its least and its largest value in every draw. col_shift takes both its least and its largest value in every draw.
All inputs are finite; a program needn't handle non-finite values.
Results may differ from the reference program's by a relative error of at most 0.0028.
Values may be sent and summed in bfloat16 or wider, within the bound.
A program may use at most 64 MiB of HBM per device.

```python
import jax
import jax.numpy as jnp
from jax import lax

W = 4096
ROWS_DEV = 64
KSIZE = 21
NBASIS = 9
DRIFT = 22
TILE = 128
HALF = 10
COL_DRIFT = 1024
SKY_ROWS = 1024
SKY_COLS = 8192
N_PATCH = 2
N_VISIT = 16


def spread_shifts(key, reach):
    first_key, second_key, third_key = jax.random.split(key, 3)
    total = N_VISIT * N_PATCH
    values = jax.random.randint(first_key, (total,), -reach, reach + 1, dtype=jnp.int32)
    first_spot = jax.random.randint(second_key, (), 0, total, dtype=jnp.int32)
    step_spot = jax.random.randint(third_key, (), 1, total, dtype=jnp.int32)
    second_spot = (first_spot + step_spot) % total
    values = values.at[first_spot].set(reach)
    values = values.at[second_spot].set(-reach)
    return values.reshape(N_VISIT, N_PATCH)


def draw_row_shift(key, part):
    return spread_shifts(key, DRIFT)


def draw_col_shift(key, part):
    return spread_shifts(jax.random.fold_in(key, 7), COL_DRIFT)


def place_ends(result, key, smallest, top_value):
    index_at = [jax.random.randint(jax.random.fold_in(key, axis), (), 0, length) for axis, length in enumerate(result.shape)]
    main_axis = result.shape.index(max(result.shape))
    beside = index_at[:main_axis] + [(index_at[main_axis] + 1) % result.shape[main_axis]] + index_at[main_axis + 1:]
    return result.at[tuple(index_at)].set(smallest).at[tuple(beside)].set(top_value)


def levels(key, shape, shards, smallest, largest):
    def one(dim, blocks):
        steps = jax.random.uniform(jax.random.fold_in(jax.random.fold_in(key, 6), dim), (blocks,), jnp.float32, smallest / len(shards), largest / len(shards))
        return jnp.repeat(jnp.exp(steps), shape[dim] // blocks).reshape((-1,) + (1,) * (len(shape) - dim - 1))

    gain = one(*shards[0])
    for cut in shards[1:]:
        gain = gain * one(*cut)
    return gain


def centred(rng, shape, spread, bound, cuts=(), kind=jnp.bfloat16):
    result = spread * jax.random.normal(rng, shape, jnp.float32)
    if cuts:
        result = result * levels(rng, shape, cuts, -0.22, 0.18)
    return jnp.clip(result, -bound, bound).astype(kind)


def setup_inputs(seed: int = 0) -> dict:
    key_list = jax.random.split(jax.random.key(seed), 9)
    return {
        "template": centred(key_list[0], (SKY_ROWS, SKY_COLS), 1.0, 6.0, ((0, 16), (1, 2))),
        "science": centred(key_list[1], (SKY_ROWS, SKY_COLS), 1.0, 6.0, ((0, 16), (1, 2))),
        "row_shift": draw_row_shift(jax.random.fold_in(key_list[8], 71), 0),
        "col_shift": draw_col_shift(jax.random.fold_in(key_list[8], 71), 0),
        "valid_rows": place_ends(jax.random.randint(key_list[4], (N_VISIT, N_PATCH), ROWS_DEV // 2, ROWS_DEV + 1), jax.random.fold_in(key_list[4], 1), ROWS_DEV // 2, ROWS_DEV).astype(jnp.int32),
        "basis_rows": centred(key_list[5], (NBASIS, KSIZE), 0.3, 2.5),
        "basis_cols": centred(key_list[6], (NBASIS, KSIZE), 0.3, 2.5),
        "kernel_terms": centred(key_list[7], (N_VISIT, N_PATCH, NBASIS), 0.4, 2.5, ((0, 16), (1, 2)), jnp.float32),
    }


def band_tables(basis_rows, basis_cols, row_count, half_kernel, tile_width):
    taps = basis_rows.shape[1]
    terms = basis_rows.shape[0]
    distance = lax.broadcasted_iota(jnp.int32, (row_count, row_count + 2 * half_kernel), 1) - lax.broadcasted_iota(jnp.int32, (row_count, row_count + 2 * half_kernel), 0)
    column_gap = lax.broadcasted_iota(jnp.int32, (tile_width + 2 * half_kernel, tile_width), 0) - lax.broadcasted_iota(jnp.int32, (tile_width + 2 * half_kernel, tile_width), 1)
    vertical_band = jnp.zeros((terms, row_count, row_count + 2 * half_kernel), jnp.float32)
    horizontal_band = jnp.zeros((terms, tile_width + 2 * half_kernel, tile_width), jnp.float32)
    for tap_index in range(taps):
        vertical_band = vertical_band + basis_rows[:, tap_index].astype(jnp.float32)[:, None, None] * (distance == tap_index).astype(jnp.float32)[None]
        horizontal_band = horizontal_band + basis_cols[:, tap_index].astype(jnp.float32)[:, None, None] * (column_gap == tap_index).astype(jnp.float32)[None]
    return vertical_band.astype(jnp.bfloat16), horizontal_band


def convolve(window, weights, vertical_band, horizontal_band, tile_width):
    row_count = vertical_band.shape[1]
    padded_cols = window.shape[1]
    twice_half = horizontal_band.shape[1] - tile_width
    col_count = padded_cols - twice_half
    tile_count = col_count // tile_width
    accumulated = jnp.zeros((row_count, tile_count, tile_width), jnp.float32)
    for basis_index in range(vertical_band.shape[0]):
        vertical = jnp.dot(vertical_band[basis_index], window, preferred_element_type=jnp.float32) * weights[basis_index]
        vertical = vertical.astype(jnp.bfloat16).astype(jnp.float32)
        extended = jnp.pad(vertical, ((0, 0), (0, (tile_count + 1) * tile_width - padded_cols)))
        blocks = extended.reshape(row_count, tile_count + 1, tile_width)
        accumulated = accumulated + jnp.einsum("rtk,kj->rtj", blocks[:, :tile_count], horizontal_band[basis_index, :tile_width], precision=lax.Precision.HIGHEST)
        accumulated = accumulated + jnp.einsum("rtk,kj->rtj", blocks[:, 1:, :twice_half], horizontal_band[basis_index, tile_width:], precision=lax.Precision.HIGHEST)
    return accumulated.reshape(row_count, col_count)


def reference(template, science, row_shift, col_shift, valid_rows, basis_rows, basis_cols, kernel_terms):
    vertical_band, horizontal_band = band_tables(basis_rows, basis_cols, ROWS_DEV, HALF, TILE)
    template_pad = jnp.pad(template, ((DRIFT + HALF, DRIFT + HALF), (COL_DRIFT + HALF, COL_DRIFT + HALF)))
    frame = jnp.zeros((SKY_ROWS + 2 * DRIFT, SKY_COLS + 2 * COL_DRIFT), jnp.float32)
    coverage = jnp.zeros((SKY_ROWS + 2 * DRIFT, SKY_COLS + 2 * COL_DRIFT), jnp.float32)
    row_index = jnp.arange(ROWS_DEV, dtype=jnp.int32)

    def one_ccd(carry, index):
        frame, coverage = carry
        visit_index = index // N_PATCH
        patch_index = index % N_PATCH
        top_row = (visit_index * ROWS_DEV + row_shift[visit_index, patch_index]).astype(jnp.int32)
        patch_start = (patch_index * W).astype(jnp.int32)
        left_col = (patch_start + col_shift[visit_index, patch_index]).astype(jnp.int32)
        window = lax.dynamic_slice(template_pad, (top_row + DRIFT, left_col + COL_DRIFT), (ROWS_DEV + 2 * HALF, W + 2 * HALF))
        pixels = lax.dynamic_slice(science, ((visit_index * ROWS_DEV).astype(jnp.int32), patch_start), (ROWS_DEV, W)).astype(jnp.float32)
        convolved = convolve(window, kernel_terms[visit_index, patch_index], vertical_band, horizontal_band, TILE)
        live_rows = row_index < valid_rows[visit_index, patch_index]
        difference = jnp.where(live_rows[:, None], pixels - convolved, jnp.float32(0.0))
        spot = (top_row + DRIFT, left_col + COL_DRIFT)
        former = lax.dynamic_slice(frame, spot, (ROWS_DEV, W))
        frame = lax.dynamic_update_slice(frame, former + difference, spot)
        counted = lax.dynamic_slice(coverage, spot, (ROWS_DEV, W))
        ones_block = jnp.broadcast_to(live_rows.astype(jnp.float32)[:, None], (ROWS_DEV, W))
        coverage = lax.dynamic_update_slice(coverage, counted + ones_block, spot)
        return (frame, coverage), None

    (frame, coverage), _ = lax.scan(one_ccd, (frame, coverage), jnp.arange(N_VISIT * N_PATCH, dtype=jnp.int32))
    summed = frame[DRIFT:DRIFT + SKY_ROWS, COL_DRIFT:COL_DRIFT + SKY_COLS]
    counts = coverage[DRIFT:DRIFT + SKY_ROWS, COL_DRIFT:COL_DRIFT + SKY_COLS]
    return summed / jnp.maximum(counts, jnp.float32(1.0))
```

```python
import functools

import jax
import jax.numpy as jnp
from jax import lax
from jax.experimental import pallas as pl
from jax.experimental.pallas import tpu as pltpu
from jax.sharding import PartitionSpec as P

DRIFT = 22
COL_DRIFT = 1024
MESH = pl.DeviceIdType.MESH
LANES = 128
TEDGE = 16
SEDGE = 32
SIDE = 24
TILE = 256
F32, BF16, I32 = jnp.float32, jnp.bfloat16, jnp.int32


def slot_of(dv, dp):
    return (dv + 1) * 3 + dp + 1


AROUND = [(dv, dp) for dv in (-1, 0, 1) for dp in (-1, 0, 1) if (dv, dp) != (0, 0)]


def plan(p, np_, chunks):
    has_left, has_right = (p > 0).astype(I32), (p < np_ - 1).astype(I32)
    passes = chunks + has_left + has_right

    def which(q):
        extra = q - chunks
        left = jnp.logical_and(extra == 0, has_left == 1)
        main = extra < 0
        c = jnp.where(main, q, jnp.where(left, 0, chunks - 1))
        dp = jnp.where(main, 0, jnp.where(left, -1, 1))
        return c, dp

    return passes, which


def kernel(
    np_, nv, template, science, row_shift, col_shift, valid_rows, basis_rows, basis_cols, terms,
    conv, moved, par_i, text, sky, par_f, sm_i, sm_f, taps, band_v, band_h, weighted,
    send_sem, recv_sem, local_sem,
):
    rows, width = template.shape
    terms_n, ksize = basis_rows.shape
    half = (ksize - 1) // 2
    group = rows + 2 * SIDE
    chunk = COL_DRIFT
    chunks = width // chunk
    tiles = chunk // TILE
    p, v = lax.axis_index("patch"), lax.axis_index("visit")

    def there(dv, dp):
        ok = None
        for cond, d in (
            (v > 0, dv == -1), (v < nv - 1, dv == 1), (p > 0, dp == -1), (p < np_ - 1, dp == 1)
        ):
            if d:
                ok = cond if ok is None else jnp.logical_and(ok, cond)
        return ok

    lane = lax.broadcasted_iota(I32, (1, LANES), 1)
    par_i[...] = jnp.zeros_like(par_i)
    par_f[...] = jnp.zeros_like(par_f)
    ints = jnp.where(
        lane == 0, row_shift[0, 0], jnp.where(lane == 1, col_shift[0, 0], jnp.where(lane == 2, valid_rows[0, 0], 0))
    )
    par_i[4] = ints
    floats = jnp.zeros((1, LANES), F32)
    for b in range(terms_n):
        floats = jnp.where(lane == b, terms[0, 0, b], floats)
    par_f[4] = floats

    own_t = pltpu.make_async_copy(
        template, text.at[pl.ds(TEDGE, rows), pl.ds(LANES, width)], local_sem.at[0]
    )
    own_s = pltpu.make_async_copy(
        science, sky.at[pl.ds(SEDGE, rows), pl.ds(COL_DRIFT, width)], local_sem.at[1]
    )
    own_t.start()
    own_s.start()

    barrier = pltpu.get_barrier_semaphore()
    for dv, dp in AROUND:
        @pl.when(there(dv, dp))
        def _():
            pl.semaphore_signal(
                barrier, inc=1, device_id={"patch": p + dp, "visit": v + dv}, device_id_type=MESH
            )
    one = lambda c: c.astype(I32)
    n_v = one(v > 0) + one(v < nv - 1)
    n_p = one(p > 0) + one(p < np_ - 1)
    pl.semaphore_wait(barrier, n_v + n_p + n_v * n_p)

    def span(d, edge, size):
        return {-1: (size - edge, 0, edge), 0: (0, edge, size), 1: (0, edge + size, edge)}[d]

    def regions(kind, dv, dp):
        if kind == 0:
            return par_i.at[4], par_i.at[slot_of(dv, dp)]
        if kind == 1:
            return par_f.at[4], par_f.at[slot_of(dv, dp)]
        src, dst, re, ce = (
            (template, text, TEDGE, LANES) if kind == 2 else (science, sky, SEDGE, COL_DRIFT)
        )
        r_src, r_dst, r_n = span(dv, re, rows)
        c_src, c_dst, c_n = span(dp, ce, width)
        return (
            src.at[pl.ds(r_src, r_n), pl.ds(c_src, c_n)],
            dst.at[pl.ds(r_dst, r_n), pl.ds(c_dst, c_n)],
        )

    def sending(kind, ev, ep):
        src, dst = regions(kind, -ev, -ep)
        return pltpu.make_async_remote_copy(
            src_ref=src, dst_ref=dst,
            send_sem=send_sem.at[kind, slot_of(ev, ep)],
            recv_sem=recv_sem.at[kind, slot_of(-ev, -ep)],
            device_id={"patch": p + ep, "visit": v + ev}, device_id_type=MESH,
        )

    def receiving(kind, dv, dp):
        _, dst = regions(kind, dv, dp)
        return pltpu.make_async_remote_copy(
            src_ref=dst, dst_ref=dst,
            send_sem=send_sem.at[kind, slot_of(dv, dp)],
            recv_sem=recv_sem.at[kind, slot_of(dv, dp)],
            device_id={"patch": p + dp, "visit": v + dv}, device_id_type=MESH,
        )

    for kinds in ((0, 1, 2), (3,)):
        for kind in kinds:
            for ev, ep in AROUND:
                @pl.when(there(ev, ep))
                def _():
                    sending(kind, ev, ep).start()

    for kind in (2, 3):
        for dv, dp in AROUND:
            @pl.when(jnp.logical_not(there(dv, dp)))
            def _():
                _, dst = regions(kind, dv, dp)
                dst[...] = jnp.zeros(dst.shape, BF16)

    taps[...] = jnp.zeros_like(taps)
    taps[0, 0:terms_n, 0:ksize] = basis_rows[...].astype(F32)
    taps[1, 0:terms_n, 0:ksize] = basis_cols[...].astype(F32)
    kk = lax.broadcasted_iota(I32, (LANES, LANES), 0)
    nn = lax.broadcasted_iota(I32, (LANES, LANES), 1)
    gap = kk - nn + half
    inside = [jnp.logical_and(gap + o >= 0, gap + o < ksize) for o in (-LANES, 0, LANES)]
    zero = jnp.zeros((LANES, LANES), BF16)
    turned_cols = pltpu.roll(taps[1], LANES - half, 1)
    for b in range(terms_n):
        row = jnp.broadcast_to(taps[0, b : b + 1, :], (rows, LANES))
        band_v[b * rows : (b + 1) * rows, :] = pltpu.roll(
            row, TEDGE - half, 1, stride=1, stride_axis=0
        ).astype(BF16)
        col = jnp.broadcast_to(turned_cols[b : b + 1, :], (LANES, LANES))
        mat = pltpu.roll(col, 0, 1, stride=1, stride_axis=0).T
        low, mid, top = [jnp.where(m, mat, 0.0).astype(BF16) for m in inside]
        at = b * TILE
        band_h[0, at : at + LANES, :] = jnp.concatenate([low, zero], axis=1)
        band_h[0, at + LANES : at + TILE, :] = jnp.concatenate([mid, low], axis=1)
        band_h[1, at : at + LANES, :] = jnp.concatenate([top, mid], axis=1)
        band_h[1, at + LANES : at + TILE, :] = jnp.concatenate([zero, top], axis=1)

    for kind in (0, 1, 2):
        for dv, dp in AROUND:
            @pl.when(there(dv, dp))
            def _():
                receiving(kind, dv, dp).wait_recv()
    to_i = pltpu.make_async_copy(par_i, sm_i, local_sem.at[2])
    to_f = pltpu.make_async_copy(par_f, sm_f, local_sem.at[3])
    to_i.start()
    to_f.start()
    own_t.wait()
    to_i.wait()
    to_f.wait()

    passes, which = plan(p, np_, chunks)

    @pl.loop(0, passes)
    def _(q):
        c, dp = which(q)
        for n in range(tiles + 1):
            start = pl.multiple_of(c * chunk + n * TILE, TILE)
            vert = jnp.dot(
                band_v[:, : rows + 2 * TEDGE], text[:, pl.ds(start, TILE)],
                preferred_element_type=F32,
            )
            for b in range(terms_n):
                mid_w = sm_f[4 + dp, 0, b]
                up_w = sm_f[1 + dp, 0, b]
                down_w = sm_f[7 + dp, 0, b]
                blk = vert[b * rows : (b + 1) * rows]
                at = n * group
                weighted[at : at + rows, b * TILE : (b + 1) * TILE] = (blk * mid_w).astype(BF16)
                weighted[at + rows : at + group, b * TILE : (b + 1) * TILE] = jnp.concatenate(
                    [blk[:SIDE] * up_w, blk[rows - SIDE :] * down_w], axis=0
                ).astype(BF16)
        conv[q] = jnp.dot(
            weighted[0 : tiles * group, :], band_h[0], preferred_element_type=F32
        ) + jnp.dot(
            weighted[group : (tiles + 1) * group, :], band_h[1], preferred_element_type=F32
        )

    own_s.wait()
    for dv, dp in AROUND:
        @pl.when(there(dv, dp))
        def _():
            receiving(3, dv, dp).wait_recv()

    def pick(dp):
        parts = []
        for dv, first, n in ((0, 0, rows), (-1, 0, SIDE), (1, rows - SIDE, SIDE)):
            y = lax.broadcasted_iota(I32, (n, rows + 2 * SEDGE), 0) + first
            j = lax.broadcasted_iota(I32, (n, rows + 2 * SEDGE), 1)
            rs = sm_i[slot_of(dv, dp), 0, 0]
            parts.append((j == y + SEDGE - rs).astype(F32))
        return jnp.concatenate(parts, axis=0).astype(BF16)

    for dp, first, n in ((-1, 0, COL_DRIFT), (0, COL_DRIFT, width), (1, COL_DRIFT + width, COL_DRIFT)):
        chosen = pick(dp)
        for k in range(n // TILE):
            at = first + k * TILE
            moved[:, at : at + TILE] = jnp.dot(
                chosen, sky[:, at : at + TILE], preferred_element_type=F32
            )

    for kind in range(4):
        for ev, ep in AROUND:
            @pl.when(there(ev, ep))
            def _():
                sending(kind, ev, ep).wait_send()


def gather_kernel(np_, conv, moved, par_i, out, count, sm_i, sem):
    rows, width = out.shape
    group = rows + 2 * SIDE
    chunk = COL_DRIFT
    chunks = width // chunk
    p = lax.axis_index("patch")
    to_i = pltpu.make_async_copy(par_i, sm_i, sem)
    to_i.start()
    out[...] = jnp.zeros_like(out)
    count[...] = jnp.zeros_like(count)
    to_i.wait()
    passes, which = plan(p, np_, chunks)

    @pl.loop(0, passes)
    def _(q):
        c, dp = which(q)
        for dv, first, n, off in (
            (0, 0, rows, 0), (-1, 0, SIDE, rows), (1, rows - SIDE, SIDE, rows + SIDE)
        ):
            slot = slot_of(dv, dp)
            rs, cs, valid = sm_i[slot, 0, 0], sm_i[slot, 0, 1], sm_i[slot, 0, 2]
            y = lax.broadcasted_iota(I32, (n, LANES), 0) + (first - dv * rows) - rs
            live = jnp.logical_and(y >= 0, y < valid)
            turn = jnp.bitwise_and(cs, LANES - 1)
            l = lax.broadcasted_iota(I32, (n, LANES), 1)
            near = l < jnp.where(turn == 0, LANES, turn)
            block = (COL_DRIFT - cs) // LANES
            base = pl.multiple_of(block * LANES + c * chunk, LANES)
            x0 = l + (c * chunk - dp * width - cs)

            def turned(k):
                return pltpu.roll(moved[off : off + n, pl.ds(base + k * LANES, LANES)], turn, 1)

            former = turned(0)
            for k in range(chunk // LANES):
                later = turned(k + 1)
                value = jnp.where(near, former, later)
                former = later
                t, h = divmod(k, TILE // LANES)
                x = x0 + k * LANES
                mask = jnp.logical_and(live, jnp.logical_and(x >= 0, x < width))
                cv = conv[q, t * group + off : t * group + off + n, h * LANES : (h + 1) * LANES]
                here = pl.ds(pl.multiple_of(c * chunk + k * LANES, LANES), LANES)
                out[first : first + n, here] += jnp.where(mask, value - cv, 0.0)
                count[first : first + n, here] += jnp.where(mask, 1.0, 0.0)

    out[...] = out[...] / jnp.maximum(count[...], 1.0)


def body(np_, nv, template, science, row_shift, col_shift, valid_rows, basis_rows, basis_cols, terms):
    rows, width = template.shape
    terms_n = basis_rows.shape[0]
    group = rows + 2 * SIDE
    tiles = COL_DRIFT // TILE
    chunks = width // COL_DRIFT
    any_ = pl.BlockSpec(memory_space=pl.ANY)
    smem = pl.BlockSpec(memory_space=pltpu.SMEM)
    vmem = pl.BlockSpec(memory_space=pltpu.VMEM)
    conv, moved, par_i = pl.pallas_call(
        functools.partial(kernel, np_, nv),
        out_shape=(
            jax.ShapeDtypeStruct((chunks + 2, tiles * group, TILE), F32),
            jax.ShapeDtypeStruct((group, width + 2 * COL_DRIFT + LANES), F32),
            jax.ShapeDtypeStruct((9, 1, LANES), I32),
        ),
        in_specs=[any_, any_, smem, smem, smem, vmem, vmem, smem],
        out_specs=(vmem, vmem, vmem),
        scratch_shapes=[
            pltpu.VMEM((rows + 2 * TEDGE, width + 2 * LANES), BF16),
            pltpu.VMEM((rows + 2 * SEDGE, width + 2 * COL_DRIFT), BF16),
            pltpu.VMEM((9, 1, LANES), F32),
            pltpu.SMEM((9, 1, LANES), I32),
            pltpu.SMEM((9, 1, LANES), F32),
            pltpu.VMEM((2, 16, LANES), F32),
            pltpu.VMEM((terms_n * rows, LANES), BF16),
            pltpu.VMEM((2, terms_n * TILE, TILE), BF16),
            pltpu.VMEM(((tiles + 1) * group, terms_n * TILE), BF16),
            pltpu.SemaphoreType.DMA((4, 9)),
            pltpu.SemaphoreType.DMA((4, 9)),
            pltpu.SemaphoreType.DMA((4,)),
        ],
        compiler_params=pltpu.CompilerParams(
            collective_id=0, has_side_effects=True, vmem_limit_bytes=40 * 1024 * 1024
        ),
    )(template, science, row_shift, col_shift, valid_rows, basis_rows, basis_cols, terms)
    return pl.pallas_call(
        functools.partial(gather_kernel, np_),
        out_shape=jax.ShapeDtypeStruct((rows, width), F32),
        in_specs=[vmem, vmem, vmem],
        out_specs=vmem,
        scratch_shapes=[
            pltpu.VMEM((rows, width), F32),
            pltpu.SMEM((9, 1, LANES), I32),
            pltpu.SemaphoreType.DMA,
        ],
        compiler_params=pltpu.CompilerParams(vmem_limit_bytes=40 * 1024 * 1024),
    )(conv, moved, par_i)


def solution(mesh):
    placed = (
        P("visit", "patch"), P("visit", "patch"), P("visit", "patch"), P("visit", "patch"),
        P("visit", "patch"), P(), P(), P("visit", "patch", None),
    )
    run = functools.partial(body, mesh.shape["patch"], mesh.shape["visit"])
    return jax.shard_map(
        run, mesh=mesh, in_specs=placed, out_specs=P("visit", "patch"), check_vma=False
    )
```

```python
import functools

import jax
import jax.numpy as jnp
from jax import lax
from jax.experimental import pallas as pl
from jax.experimental.pallas import tpu as pltpu
from jax.sharding import PartitionSpec as P

DRIFT = 22
COL_DRIFT = 1024
MESH = pl.DeviceIdType.MESH
LANES = 128
TEDGE = 16
SEDGE = 32
SIDE = 24
TILE = 256
F32, BF16, I32 = jnp.float32, jnp.bfloat16, jnp.int32


def slot_of(dv, dp):
    return (dv + 1) * 3 + dp + 1


AROUND = [(dv, dp) for dv in (-1, 0, 1) for dp in (-1, 0, 1) if (dv, dp) != (0, 0)]


def plan(p, np_, chunks):
    has_left, has_right = (p > 0).astype(I32), (p < np_ - 1).astype(I32)
    passes = chunks + has_left + has_right

    def which(q):
        extra = q - chunks
        left = jnp.logical_and(extra == 0, has_left == 1)
        main = extra < 0
        c = jnp.where(main, q, jnp.where(left, 0, chunks - 1))
        dp = jnp.where(main, 0, jnp.where(left, -1, 1))
        return c, dp

    return passes, which


def kernel(
    np_, nv, template, science, row_shift, col_shift, valid_rows, basis_rows_hbm, basis_cols_hbm,
    terms_hbm, conv, moved, par_i, basis_rows, basis_cols, terms, text, sky, par_f, sm_i, sm_f, taps, band_v, band_h, weighted,
    conv_v, moved_v, par_v, send_sem, recv_sem, local_sem, out_sem,
):
    rows, width = template.shape
    terms_n, ksize = basis_rows.shape
    half = (ksize - 1) // 2
    group = rows + 2 * SIDE
    chunk = COL_DRIFT
    chunks = width // chunk
    tiles = chunk // TILE
    p, v = lax.axis_index("patch"), lax.axis_index("visit")

    def there(dv, dp):
        ok = None
        for cond, d in (
            (v > 0, dv == -1), (v < nv - 1, dv == 1), (p > 0, dp == -1), (p < np_ - 1, dp == 1)
        ):
            if d:
                ok = cond if ok is None else jnp.logical_and(ok, cond)
        return ok

    small = [
        pltpu.make_async_copy(a, b, local_sem.at[4 + i])
        for i, (a, b) in enumerate(
            ((terms_hbm, terms), (basis_rows_hbm, basis_rows), (basis_cols_hbm, basis_cols))
        )
    ]
    for copy in small:
        copy.start()
    lane = lax.broadcasted_iota(I32, (1, LANES), 1)
    par_v[...] = jnp.zeros_like(par_v)
    par_f[...] = jnp.zeros_like(par_f)
    ints = jnp.where(
        lane == 0, row_shift[0, 0], jnp.where(lane == 1, col_shift[0, 0], jnp.where(lane == 2, valid_rows[0, 0], 0))
    )
    par_v[4] = ints
    own_t = pltpu.make_async_copy(
        template, text.at[pl.ds(TEDGE, rows), pl.ds(LANES, width)], local_sem.at[0]
    )
    own_s = pltpu.make_async_copy(
        science, sky.at[pl.ds(SEDGE, rows), pl.ds(COL_DRIFT, width)], local_sem.at[1]
    )
    own_t.start()
    own_s.start()
    small[0].wait()
    par_f[4, :, 0:terms_n] = terms[0]

    barrier = pltpu.get_barrier_semaphore()
    for dv, dp in AROUND:
        @pl.when(there(dv, dp))
        def _():
            pl.semaphore_signal(
                barrier, inc=1, device_id={"patch": p + dp, "visit": v + dv}, device_id_type=MESH
            )
    one = lambda c: c.astype(I32)
    n_v = one(v > 0) + one(v < nv - 1)
    n_p = one(p > 0) + one(p < np_ - 1)
    pl.semaphore_wait(barrier, n_v + n_p + n_v * n_p)

    def span(d, edge, size):
        return {-1: (size - edge, 0, edge), 0: (0, edge, size), 1: (0, edge + size, edge)}[d]

    def regions(kind, dv, dp):
        if kind == 0:
            return par_v.at[4], par_v.at[slot_of(dv, dp)]
        if kind == 1:
            return par_f.at[4], par_f.at[slot_of(dv, dp)]
        src, dst, re, ce = (
            (template, text, TEDGE, LANES) if kind == 2 else (science, sky, SEDGE, COL_DRIFT)
        )
        r_src, r_dst, r_n = span(dv, re, rows)
        c_src, c_dst, c_n = span(dp, ce, width)
        return (
            src.at[pl.ds(r_src, r_n), pl.ds(c_src, c_n)],
            dst.at[pl.ds(r_dst, r_n), pl.ds(c_dst, c_n)],
        )

    def sending(kind, ev, ep):
        src, dst = regions(kind, -ev, -ep)
        return pltpu.make_async_remote_copy(
            src_ref=src, dst_ref=dst,
            send_sem=send_sem.at[kind, slot_of(ev, ep)],
            recv_sem=recv_sem.at[kind, slot_of(-ev, -ep)],
            device_id={"patch": p + ep, "visit": v + ev}, device_id_type=MESH,
        )

    def receiving(kind, dv, dp):
        _, dst = regions(kind, dv, dp)
        return pltpu.make_async_remote_copy(
            src_ref=dst, dst_ref=dst,
            send_sem=send_sem.at[kind, slot_of(dv, dp)],
            recv_sem=recv_sem.at[kind, slot_of(dv, dp)],
            device_id={"patch": p + dp, "visit": v + dv}, device_id_type=MESH,
        )

    def send_all(kind):
        for ev, ep in AROUND:
            @pl.when(there(ev, ep))
            def _():
                sending(kind, ev, ep).start()

    for kind in (0, 1, 2):
        send_all(kind)

    for kind in (2, 3):
        for dv, dp in AROUND:
            @pl.when(jnp.logical_not(there(dv, dp)))
            def _():
                _, dst = regions(kind, dv, dp)
                dst[...] = jnp.zeros(dst.shape, BF16)

    small[1].wait()
    small[2].wait()
    taps[...] = jnp.zeros_like(taps)
    taps[0, 0:terms_n, 0:ksize] = basis_rows[...].astype(F32)
    taps[1, 0:terms_n, 0:ksize] = basis_cols[...].astype(F32)
    kk = lax.broadcasted_iota(I32, (LANES, LANES), 0)
    nn = lax.broadcasted_iota(I32, (LANES, LANES), 1)
    gap = kk - nn + half
    inside = [jnp.logical_and(gap + o >= 0, gap + o < ksize) for o in (-LANES, 0, LANES)]
    zero = jnp.zeros((LANES, LANES), BF16)
    turned_cols = pltpu.roll(taps[1], LANES - half, 1)
    for b in range(terms_n):
        row = jnp.broadcast_to(taps[0, b : b + 1, :], (rows, LANES))
        band_v[b * rows : (b + 1) * rows, :] = pltpu.roll(
            row, TEDGE - half, 1, stride=1, stride_axis=0
        ).astype(BF16)
        col = jnp.broadcast_to(turned_cols[b : b + 1, :], (LANES, LANES))
        mat = pltpu.roll(col, 0, 1, stride=1, stride_axis=0).T
        low, mid, top = [jnp.where(m, mat, 0.0).astype(BF16) for m in inside]
        at = b * TILE
        band_h[0, at : at + LANES, :] = jnp.concatenate([low, zero], axis=1)
        band_h[0, at + LANES : at + TILE, :] = jnp.concatenate([mid, low], axis=1)
        band_h[1, at : at + LANES, :] = jnp.concatenate([top, mid], axis=1)
        band_h[1, at + LANES : at + TILE, :] = jnp.concatenate([zero, top], axis=1)

    for kind in (0, 1, 2):
        for dv, dp in AROUND:
            @pl.when(there(dv, dp))
            def _():
                receiving(kind, dv, dp).wait_recv()
    send_all(3)
    to_i = pltpu.make_async_copy(par_v, sm_i, local_sem.at[2])
    to_f = pltpu.make_async_copy(par_f, sm_f, local_sem.at[3])
    to_i.start()
    to_f.start()
    own_t.wait()
    to_i.wait()
    to_f.wait()

    passes, which = plan(p, np_, chunks)

    @pl.loop(0, passes)
    def _(q):
        c, dp = which(q)
        for n in range(tiles + 1):
            start = pl.multiple_of(c * chunk + n * TILE, TILE)
            vert = jnp.dot(
                band_v[:, : rows + 2 * TEDGE], text[:, pl.ds(start, TILE)],
                preferred_element_type=F32,
            )
            for b in range(terms_n):
                mid_w = sm_f[4 + dp, 0, b]
                up_w = sm_f[1 + dp, 0, b]
                down_w = sm_f[7 + dp, 0, b]
                blk = vert[b * rows : (b + 1) * rows]
                at = n * group
                weighted[at : at + rows, b * TILE : (b + 1) * TILE] = (blk * mid_w).astype(BF16)
                weighted[at + rows : at + group, b * TILE : (b + 1) * TILE] = jnp.concatenate(
                    [blk[:SIDE] * up_w, blk[rows - SIDE :] * down_w], axis=0
                ).astype(BF16)
        conv_v[q] = jnp.dot(
            weighted[0 : tiles * group, :], band_h[0], preferred_element_type=F32
        ) + jnp.dot(
            weighted[group : (tiles + 1) * group, :], band_h[1], preferred_element_type=F32
        )
        pltpu.make_async_copy(conv_v.at[q], conv.at[q], out_sem.at[q]).start()

    own_s.wait()
    for dv, dp in AROUND:
        @pl.when(there(dv, dp))
        def _():
            receiving(3, dv, dp).wait_recv()

    def pick(dp):
        parts = []
        for dv, first, n in ((0, 0, rows), (-1, 0, SEDGE), (1, rows - SEDGE, SEDGE)):
            y = lax.broadcasted_iota(I32, (n, rows + 2 * SEDGE), 0) + first
            j = lax.broadcasted_iota(I32, (n, rows + 2 * SEDGE), 1)
            rs = sm_i[slot_of(dv, dp), 0, 0]
            parts.append((j == y + SEDGE - rs).astype(F32))
        return jnp.concatenate(parts, axis=0).astype(BF16)

    par_out = pltpu.make_async_copy(par_v, par_i, local_sem.at[2])
    par_out.start()
    leaving = [par_out]
    halfway = width // 2
    for i, (dp, first, n) in enumerate((
        (-1, 0, COL_DRIFT), (0, COL_DRIFT, halfway), (0, COL_DRIFT + halfway, halfway),
        (1, COL_DRIFT + width, COL_DRIFT),
    )):
        chosen = pick(dp)
        for t in range(n // TILE):
            at = first + t * TILE
            moved_v[:, at : at + TILE] = jnp.dot(
                chosen, sky[:, at : at + TILE], preferred_element_type=F32
            ).astype(BF16)
        part = (slice(None), pl.ds(first, n))
        copy = pltpu.make_async_copy(moved_v.at[part], moved.at[part], out_sem.at[chunks + 2 + i])
        copy.start()
        leaving.append(copy)

    for kind in range(4):
        for ev, ep in AROUND:
            @pl.when(there(ev, ep))
            def _():
                sending(kind, ev, ep).wait_send()
    for copy in leaving:
        copy.wait()

    @pl.loop(0, passes)
    def _(q):
        pltpu.make_async_copy(conv_v.at[q], conv.at[q], out_sem.at[q]).wait()


def gather_kernel(
    np_, conv_h, moved_h, par_i, out_h, conv, moved, out, count, sm_i, sem, conv_sem, moved_sem, out_sem
):
    rows, width = out_h.shape
    group = rows + 2 * SIDE
    chunk = COL_DRIFT
    chunks = width // chunk
    p = lax.axis_index("patch")
    to_i = pltpu.make_async_copy(par_i, sm_i, sem)
    to_i.start()
    bring = []
    halfway = width // 2
    for i, (first, n) in enumerate((
        (0, chunk), (chunk, halfway), (chunk + halfway, halfway), (chunk + width, chunk)
    )):
        part = (slice(None), pl.ds(first, n))
        bring.append(pltpu.make_async_copy(moved_h.at[part], moved.at[part], moved_sem.at[i]))
        bring[-1].start()
    passes, which = plan(p, np_, chunks)

    @pl.loop(0, passes)
    def _(q):
        pltpu.make_async_copy(conv_h.at[q], conv.at[q], conv_sem.at[q]).start()

    out[...] = jnp.zeros_like(out)
    count[...] = jnp.zeros_like(count)
    to_i.wait()
    for copy in bring:
        copy.wait()

    @pl.loop(0, passes)
    def _(q):
        c, dp = which(q)
        pltpu.make_async_copy(conv_h.at[q], conv.at[q], conv_sem.at[q]).wait()
        for dv, first, n, off in (
            (0, 0, rows, 0), (-1, 0, SIDE, rows), (1, rows - SIDE, SIDE, rows + SIDE)
        ):
            slot = slot_of(dv, dp)
            rs, cs, valid = sm_i[slot, 0, 0], sm_i[slot, 0, 1], sm_i[slot, 0, 2]
            y = lax.broadcasted_iota(I32, (n, LANES), 0) + (first - dv * rows) - rs
            live = jnp.logical_and(y >= 0, y < valid)
            src, src_n = {0: (0, rows), -1: (rows, SEDGE), 1: (rows + SEDGE, SEDGE)}[dv]
            skip = SEDGE - SIDE if dv == 1 else 0
            turn = jnp.bitwise_and(cs, LANES - 1)
            l = lax.broadcasted_iota(I32, (n, LANES), 1)
            near = l < jnp.where(turn == 0, LANES, turn)
            block = (COL_DRIFT - cs) // LANES
            base = pl.multiple_of(block * LANES + c * chunk, LANES)
            x0 = l + (c * chunk - dp * width - cs)

            def turned(k):
                got = moved[src : src + src_n, pl.ds(base + k * LANES, LANES)].astype(F32)
                return pltpu.roll(got[skip : skip + n], turn, 1)

            former = turned(0)
            for k in range(chunk // LANES):
                later = turned(k + 1)
                value = jnp.where(near, former, later)
                former = later
                t, h = divmod(k, TILE // LANES)
                x = x0 + k * LANES
                mask = jnp.logical_and(live, jnp.logical_and(x >= 0, x < width))
                cv = conv[q, t * group + off : t * group + off + n, h * LANES : (h + 1) * LANES]
                here = pl.ds(pl.multiple_of(c * chunk + k * LANES, LANES), LANES)
                out[first : first + n, here] += jnp.where(mask, value - cv, 0.0)
                count[first : first + n, here] += jnp.where(mask, 1.0, 0.0)

    leaving = []
    for c in range(chunks):
        part = (slice(None), pl.ds(c * chunk, chunk))
        out[part] = out[part] / jnp.maximum(count[part], 1.0)
        leaving.append(pltpu.make_async_copy(out.at[part], out_h.at[part], out_sem.at[c]))
        leaving[-1].start()
    for copy in leaving:
        copy.wait()


def body(np_, nv, template, science, row_shift, col_shift, valid_rows, basis_rows, basis_cols, terms):
    rows, width = template.shape
    terms_n = basis_rows.shape[0]
    group = rows + 2 * SIDE
    tiles = COL_DRIFT // TILE
    chunks = width // COL_DRIFT
    hbm = pl.BlockSpec(memory_space=pltpu.HBM)
    smem = pl.BlockSpec(memory_space=pltpu.SMEM)
    conv, moved, par_i = pl.pallas_call(
        functools.partial(kernel, np_, nv),
        out_shape=(
            jax.ShapeDtypeStruct((chunks + 2, tiles * group, TILE), F32),
            jax.ShapeDtypeStruct((rows + 2 * SEDGE, width + 2 * COL_DRIFT + LANES), BF16),
            jax.ShapeDtypeStruct((9, 1, LANES), I32),
        ),
        in_specs=[hbm, hbm, smem, smem, smem, hbm, hbm, hbm],
        out_specs=(hbm, hbm, hbm),
        scratch_shapes=[
            pltpu.VMEM(basis_rows.shape, BF16),
            pltpu.VMEM(basis_cols.shape, BF16),
            pltpu.VMEM(terms.shape, F32),
            pltpu.VMEM((rows + 2 * TEDGE, width + 2 * LANES), BF16),
            pltpu.VMEM((rows + 2 * SEDGE, width + 2 * COL_DRIFT), BF16),
            pltpu.VMEM((9, 1, LANES), F32),
            pltpu.SMEM((9, 1, LANES), I32),
            pltpu.SMEM((9, 1, LANES), F32),
            pltpu.VMEM((2, 16, LANES), F32),
            pltpu.VMEM((terms_n * rows, LANES), BF16),
            pltpu.VMEM((2, terms_n * TILE, TILE), BF16),
            pltpu.VMEM(((tiles + 1) * group, terms_n * TILE), BF16),
            pltpu.VMEM((chunks + 2, tiles * group, TILE), F32),
            pltpu.VMEM((rows + 2 * SEDGE, width + 2 * COL_DRIFT + LANES), BF16),
            pltpu.VMEM((9, 1, LANES), I32),
            pltpu.SemaphoreType.DMA((4, 9)),
            pltpu.SemaphoreType.DMA((4, 9)),
            pltpu.SemaphoreType.DMA((7,)),
            pltpu.SemaphoreType.DMA((chunks + 6,)),
        ],
        compiler_params=pltpu.CompilerParams(
            collective_id=0, has_side_effects=True, vmem_limit_bytes=58 * 1024 * 1024
        ),
    )(template, science, row_shift, col_shift, valid_rows, basis_rows, basis_cols, terms)
    return pl.pallas_call(
        functools.partial(gather_kernel, np_),
        out_shape=jax.ShapeDtypeStruct((rows, width), F32),
        in_specs=[hbm, hbm, hbm],
        out_specs=hbm,
        scratch_shapes=[
            pltpu.VMEM((chunks + 2, tiles * group, TILE), F32),
            pltpu.VMEM((rows + 2 * SEDGE, width + 2 * COL_DRIFT + LANES), BF16),
            pltpu.VMEM((rows, width), F32),
            pltpu.VMEM((rows, width), F32),
            pltpu.SMEM((9, 1, LANES), I32),
            pltpu.SemaphoreType.DMA,
            pltpu.SemaphoreType.DMA((chunks + 2,)),
            pltpu.SemaphoreType.DMA((4,)),
            pltpu.SemaphoreType.DMA((chunks,)),
        ],
        compiler_params=pltpu.CompilerParams(vmem_limit_bytes=58 * 1024 * 1024),
    )(conv, moved, par_i)


def solution(mesh):
    placed = (
        P("visit", "patch"), P("visit", "patch"), P("visit", "patch"), P("visit", "patch"),
        P("visit", "patch"), P(), P(), P("visit", "patch", None),
    )
    run = functools.partial(body, mesh.shape["patch"], mesh.shape["visit"])
    return jax.shard_map(
        run, mesh=mesh, in_specs=placed, out_specs=P("visit", "patch"), check_vma=False
    )
```
